512 devices in a mesh: chan: 64 (over y_hi, z, core), win: 8 (over x, y_lo).
Axes of the slice: x: 4, y: 8 (y_hi: 4, y_lo: 2; y = y_hi * 2 + y_lo), z: 8, core: 2. Of those that a mesh axis runs over, the one named last changes fastest.
Arguments:
- strain: bfloat16 [2048, 8, 15000], P('chan', 'win'), may hold values from -6 to 6
- gaps: int32 [2048, 8], P('chan', 'win'), may hold values 0 or 1
- source_block: int32 [1], replicated, may hold values from 0 to 32767
Outputs:
- stacks: float32 [64, 2048, 256], P('win', 'chan')
The draws below stay inside these ranges and needn't reach their ends.
Inputs may be any that keep to these rules, and one draw needn't show every extreme that they name: The plan's step number; the block of 64 channels used as virtual sources is source_block[0] mod 32. `gaps`: 1 where a channel's segment is usable, 0 where it holds a gap or glitch.
All inputs are finite; a program needn't handle non-finite values. No bound on the sum of `gaps` on one device may be relied on, other than what follows from the above.
Results may differ from the reference program's by a relative error of at most 0.01.
Values may be sent and summed in bfloat16 or wider, within the bound.
No kernel may reach another device: no remote copies, remote signals or barrier semaphores. Data moves between devices by JAX's collectives and lax.ppermute only.
A program may use at most 64 MiB of HBM per device.

```python
import math
import jax
import jax.numpy as jnp
from jax import lax

SAMPLES = 15000
NB = 1280
LAGS = 256
SRC = 64
SEG_DEV = 1
CHANNELS = 2048
SEGS = 8
BLOCKS = 32
N_WIN = 8


def with_ends(array, stream_key, least, top_value):
    place = [jax.random.randint(jax.random.fold_in(stream_key, axis), (), 0, length) for axis, length in enumerate(array.shape)]
    longest = array.shape.index(max(array.shape))
    beside = place[:longest] + [(place[longest] + 1) % array.shape[longest]] + place[longest + 1:]
    return array.at[tuple(place)].set(least).at[tuple(beside)].set(top_value)


def level_of(rng, shape, split, smallest, largest):
    gain, own = 1.0, jax.random.fold_in(rng, 6)
    for position, blocks in split:
        draws = jnp.exp(jax.random.uniform(jax.random.fold_in(own, position), (blocks,), jnp.float32, smallest / len(split), largest / len(split)))
        gain = gain * jnp.repeat(draws, shape[position] // blocks).reshape([-1 if axis == position else 1 for axis in range(len(shape))])
    return gain


def gaussian(key, extent, width, reach, shards=(), kind=jnp.bfloat16):
    array = width * jax.random.normal(key, extent, jnp.float32)
    if shards:
        array = array * level_of(key, extent, shards, -0.22, 0.18)
    return jnp.clip(array, -reach, reach).astype(kind)


def setup_inputs(seed: int = 0) -> dict:
    streams_of = jax.random.split(jax.random.key(seed), 4)
    return {
        "strain": gaussian(streams_of[0], (CHANNELS, SEGS, SAMPLES), 1.0, 6.0, ((0, 64), (1, 8))),
        "gaps": with_ends((jax.random.randint(streams_of[1], (CHANNELS, SEGS), 0, 8) < 7).astype(jnp.int32), jax.random.fold_in(streams_of[1], 1), 0, 1),
        "source_block": jax.random.randint(streams_of[2], (1,), 0, 1024 * BLOCKS).astype(jnp.int32),
    }


def whiten_rows(rows, flags):
    spectrum = jnp.fft.rfft(rows.astype(jnp.float32), axis=-1)[:, :NB + 64]
    spectrum_real = jnp.real(spectrum).astype(jnp.float32)
    spectrum_imag = jnp.imag(spectrum).astype(jnp.float32)
    magnitude = jnp.sqrt(spectrum_real * spectrum_real + spectrum_imag * spectrum_imag)
    level = lax.reduce_window(magnitude, jnp.zeros((), magnitude.dtype), lax.add, (1, 65), (1, 1), 'VALID') / 65.0
    factor = flags.astype(jnp.float32)[:, None] / (level + 1e-06)
    real_part = (spectrum_real[:, 32:32 + NB] * factor).astype(jnp.bfloat16)
    imag_part = (spectrum_imag[:, 32:32 + NB] * factor).astype(jnp.bfloat16)
    return jnp.stack([real_part, imag_part])

def lag_table():
    frequency = 32 + jnp.arange(NB, dtype=jnp.int32)
    offset = jnp.arange(LAGS, dtype=jnp.int32) - LAGS // 2 + SAMPLES
    phase = (frequency[:, None] * offset[None, :] % SAMPLES).astype(jnp.float32) * (2.0 * math.pi / SAMPLES)
    return jnp.concatenate([jnp.cos(phase), -jnp.sin(phase)], axis=0).astype(jnp.bfloat16)

def lag_term(mine, theirs, table, scale):
    mine_wide = mine.astype(jnp.float32)
    theirs_wide = theirs.astype(jnp.float32)
    high = lax.Precision.HIGHEST
    real_part = jnp.einsum('rgf,sgf->srf', mine_wide[0], theirs_wide[0], precision=high) + jnp.einsum('rgf,sgf->srf', mine_wide[1], theirs_wide[1], precision=high)
    imag_part = jnp.einsum('rgf,sgf->srf', mine_wide[1], theirs_wide[0], precision=high) - jnp.einsum('rgf,sgf->srf', mine_wide[0], theirs_wide[1], precision=high)
    cross = jnp.concatenate([real_part, imag_part], axis=-1).astype(jnp.bfloat16)
    count_src, count_rec = (cross.shape[0], cross.shape[1])
    lagged = jnp.dot(cross.reshape(count_src * count_rec, 2 * NB), table, preferred_element_type=jnp.float32)
    return lagged.reshape(count_src, count_rec, LAGS) * scale

def reference(strain, gaps, source_block):

    def whiten_block(pair):
        block_strain, block_gaps = pair
        flat = whiten_rows(block_strain.reshape(SRC * SEGS, SAMPLES), block_gaps.reshape(SRC * SEGS))
        return flat.reshape(2, SRC, SEGS, NB)
    whitened = lax.map(whiten_block, (strain.reshape(BLOCKS, SRC, SEGS, SAMPLES), gaps.reshape(BLOCKS, SRC, SEGS)))
    start = (source_block[0].astype(jnp.int32) % BLOCKS).astype(jnp.int32) * SRC
    sources = lax.dynamic_slice_in_dim(jnp.moveaxis(whitened, 1, 0).reshape(2, CHANNELS, SEGS, NB), start, SRC, 1)
    table = lag_table()
    scale = 1.0 / math.sqrt(NB * SEGS)

    def stack_block(block_spectra):
        total = jnp.zeros((SRC, SRC, LAGS), jnp.float32)
        for group in range(N_WIN):
            lower = group * SEG_DEV
            total = total + lag_term(block_spectra[:, :, lower:lower + SEG_DEV], sources[:, :, lower:lower + SEG_DEV], table, scale)
        return total
    result = lax.map(stack_block, whitened)
    return jnp.transpose(result, (1, 0, 2, 3)).reshape(SRC, CHANNELS, LAGS)
```

```python
import math

import jax
import jax.numpy as jnp
import numpy as np
from jax import lax
from jax.experimental import pallas as pl
from jax.experimental.pallas import tpu as pltpu
from jax.sharding import Mesh
from jax.sharding import PartitionSpec as P

SAMPLES = 15000
NB = 1280
LAGS = 256
SRC = 64
RADIX = 12
PART = SAMPLES // RADIX
PART_PAD = 1280
BINS = 112
LANES = 128
HALF_ROOT3 = math.sqrt(3.0) / 2.0

F32 = jnp.float32
BF16 = jnp.bfloat16


def piece_count(start):
    return (NB - 1 - start) // RADIX + 1


OFFSETS = [sum(piece_count(s) for s in range(start)) for start in range(RADIX + 1)]


def frequency_order():
    return np.concatenate([start + RADIX * np.arange(piece_count(start)) for start in range(RADIX)])


def transform_tables():
    sample = np.arange(PART_PAD)
    residue = np.arange(RADIX)
    angle = 2.0 * np.pi * ((residue[:, None] * sample[None, :]) % SAMPLES) / SAMPLES
    twiddle = np.stack([np.cos(angle), np.sin(angle)], axis=1).reshape(2 * RADIX, PART_PAD)
    upper = np.arange(BINS)
    angle = 2.0 * np.pi * ((sample[:, None] * upper[None, :]) % PART) / PART
    keep = (sample < PART)[:, None]
    full = np.zeros((PART_PAD, 2 * LANES))
    full[:, :BINS] = np.cos(angle) * keep
    full[:, LANES : LANES + BINS] = np.sin(angle) * keep
    high = full.astype(np.float32).astype(BF16)
    low = (full - high.astype(np.float64)).astype(np.float32).astype(BF16)
    return twiddle.astype(np.float32), high, low


def lag_table():
    frequency = 32 + frequency_order()
    offset = np.arange(LAGS) - LAGS // 2 + SAMPLES
    phase = 2.0 * np.pi * ((frequency[:, None] * offset[None, :]) % SAMPLES) / SAMPLES
    blocks = NB // LANES
    real = np.cos(phase).reshape(blocks, 1, LANES, LAGS)
    imag = -np.sin(phase).reshape(blocks, 1, LANES, LAGS)
    table = np.concatenate([real, imag], axis=1).reshape(2 * NB, LAGS)
    return table.astype(np.float32).astype(BF16)


def real_radix12(x):
    even = [None] + [x[q] + x[RADIX - q] for q in range(1, 6)]
    odd = [None] + [x[q] - x[RADIX - q] for q in range(1, 6)]
    sum06, dif06 = x[0] + x[6], x[0] - x[6]
    e15p, e15m, e24p, e24m = even[1] + even[5], even[1] - even[5], even[2] + even[4], even[2] - even[4]
    o15p, o15m, o24p, o24m = odd[1] + odd[5], odd[1] - odd[5], odd[2] + odd[4], odd[2] - odd[4]
    c, h = HALF_ROOT3, 0.5
    real = [
        sum06 + e15p + e24p + even[3],
        dif06 + c * e15m + h * e24m,
        sum06 + h * (e15p - e24p) - even[3],
        dif06 - e24m,
        sum06 - h * (e15p + e24p) + even[3],
        dif06 - c * e15m + h * e24m,
        sum06 - e15p + e24p - even[3],
    ]
    imag = [
        None,
        -(h * o15p + c * o24p + odd[3]),
        -c * (o15m + o24m),
        odd[3] - o15p,
        -c * (o15m - o24m),
        c * o24p - h * o15p - odd[3],
        None,
    ]
    return real, imag


def row_of(residue, part):
    return 0 if residue == 0 else 32 * (2 * residue - 1 + part)


def roll(value, shift, axis):
    size = value.shape[axis]
    shift = shift % size
    return value if shift == 0 else pltpu.roll(value, shift, axis)


def spectra_kernel(x_ref, gaps_ref, tw_ref, high_ref, low_ref, w_ref, s_ref, tail, a_ref, p_ref):
    blocks = PART_PAD // LANES
    last = SAMPLES // LANES * LANES
    lane16 = lax.broadcasted_iota(jnp.int32, (16, LANES), 1)
    tail[...] = jnp.zeros_like(tail)
    tail[:, : SAMPLES - last] = x_ref[:, last:].astype(F32)

    for half in range(2):
        rows = slice(16 * half, 16 * half + 16)
        held = {}

        def shifted(q, place):
            if (q, place) not in held:
                start = (q * PART // LANES + place) * LANES
                if start >= last:
                    raw = tail[rows, :]
                else:
                    raw = x_ref[rows, start : start + LANES].astype(F32)
                held[(q, place)] = roll(raw, -(q * PART % LANES), 1)
            return held[(q, place)]

        for block in range(blocks):
            parts = []
            for q in range(RADIX):
                turn = q * PART % LANES
                now = shifted(q, block)
                if turn and not (q == RADIX - 1 and block == blocks - 1):
                    now = jnp.where(lane16 < LANES - turn, now, shifted(q, block + 1))
                elif turn:
                    now = jnp.where(lane16 < LANES - turn, now, shifted(q, block + 1))
                parts.append(now)
            real, imag = real_radix12(parts)
            columns = slice(LANES * block, LANES * (block + 1))
            wide = slice(PART_PAD + LANES * block, PART_PAD + LANES * (block + 1))

            def keep(value, residue, part):
                at = row_of(residue, part) + 16 * half
                high = value.astype(BF16)
                a_ref[at : at + 16, columns] = high
                a_ref[at : at + 16, wide] = (value - high.astype(F32)).astype(BF16)

            keep(real[0], 0, 0)
            for residue in range(1, RADIX):
                base = min(residue, RADIX - residue)
                re, im = real[base], imag[base]
                cosine = tw_ref[2 * residue : 2 * residue + 1, columns]
                sine = tw_ref[2 * residue + 1 : 2 * residue + 2, columns]
                if im is None:
                    keep(re * cosine, residue, 0)
                    keep(-(re * sine), residue, 1)
                elif residue < 6:
                    keep(re * cosine + im * sine, residue, 0)
                    keep(im * cosine - re * sine, residue, 1)
                else:
                    keep(re * cosine - im * sine, residue, 0)
                    keep(-(im * cosine) - re * sine, residue, 1)

    p_ref[...] = (
        jnp.dot(a_ref[:, :PART_PAD], high_ref[...], preferred_element_type=F32)
        + jnp.dot(a_ref[:, PART_PAD:], high_ref[...], preferred_element_type=F32)
        + jnp.dot(a_ref[:, :PART_PAD], low_ref[...], preferred_element_type=F32)
    )

    lane = lax.broadcasted_iota(jnp.int32, (8, LANES), 1)
    row = lax.broadcasted_iota(jnp.int32, (8, LANES), 0)
    flat = []
    for group in range(4):
        first = 8 * group
        re, im, mag = [], [], []
        for residue in range(RADIX):
            at = row_of(residue, 0) + first
            real = p_ref[at : at + 8, :LANES]
            imag = -p_ref[at : at + 8, LANES:]
            if residue:
                other = row_of(residue, 1) + first
                real = real + p_ref[other : other + 8, LANES:]
                imag = imag + p_ref[other : other + 8, :LANES]
            re.append(real)
            im.append(imag)
            mag.append(jnp.sqrt(real * real + imag * imag))
        five, five_next, sixth, sixth_next = [], [], [], []
        for residue in range(RADIX):
            m = mag[residue]
            two = m + roll(m, -1, 1)
            four = two + roll(two, -2, 1)
            total = four + roll(m, -4, 1)
            five.append(total)
            five_next.append(roll(total, -1, 1))
            sixth.append(roll(m, -5, 1))
            sixth_next.append(roll(m, -6, 1) if residue < 4 else None)
        after = [None] * (RADIX + 1)
        for start in range(RADIX - 1, -1, -1):
            after[start] = five[start] if after[start + 1] is None else after[start + 1] + five[start]
        gap = gaps_ref[first : first + 8, :].astype(F32)
        before = None
        out = [[None] * (NB // LANES), [None] * (NB // LANES)]
        for start in range(RADIX):
            level = after[start] if before is None else after[start] + before
            for extra in range(start, start + 5):
                level = level + (sixth[extra] if extra < RADIX else sixth_next[extra - RADIX])
            before = five_next[start] if before is None else before + five_next[start]
            factor = gap / (level / 65.0 + 1e-06)
            residue = start - 4 if start >= 4 else start + 8
            shift = 3 if start >= 4 else 2
            factor = roll(factor, shift, 1)
            offset = OFFSETS[start]
            end = OFFSETS[start + 1]
            for part, spectrum in enumerate((re, im)):
                piece = roll(spectrum[residue] * factor, offset - shift, 1)
                for block in range(offset // LANES, (end - 1) // LANES + 1):
                    low = max(offset - block * LANES, 0)
                    if out[part][block] is None:
                        out[part][block] = piece
                    else:
                        out[part][block] = jnp.where(lane >= low, piece, out[part][block])
        flat.append(out[0] + out[1])

    columns = 2 * NB // LANES
    for block in range(columns):
        for half in range(2):
            pair = jnp.concatenate([flat[2 * half][block], flat[2 * half + 1][block]], axis=0)
            w_ref[16 * half : 16 * half + 16, LANES * block : LANES * (block + 1)] = pair.astype(BF16)
    each = columns // 4
    for member in range(4):
        mixed = []
        for block in range(columns):
            value = None
            for group in range(4):
                turned = roll(flat[group][block], 2 * group - 2 * member, 0)
                value = turned if value is None else jnp.where(row >= 2 * group, turned, value)
            mixed.append(value)
        for pair in range(2):
            at = 32 * member + 16 * pair
            for block in range(each):
                both = jnp.concatenate([mixed[2 * pair * each + block], mixed[(2 * pair + 1) * each + block]], axis=0)
                s_ref[at : at + 16, LANES * block : LANES * (block + 1)] = both.astype(BF16)


def spectra(strain, gaps):
    twiddle, high, low = transform_tables()
    return pl.pallas_call(
        spectra_kernel,
        out_shape=(
            jax.ShapeDtypeStruct((32, 2 * NB), BF16),
            jax.ShapeDtypeStruct((128, 640), BF16),
        ),
        scratch_shapes=[
            pltpu.VMEM((32, LANES), F32),
            pltpu.VMEM((23 * 32, 2 * PART_PAD), BF16),
            pltpu.VMEM((23 * 32, 2 * LANES), F32),
        ],
        compiler_params=pltpu.CompilerParams(vmem_limit_bytes=40 * 1024 * 1024),
        name="spectra",
    )(strain, gaps, jnp.asarray(twiddle), jnp.asarray(high), jnp.asarray(low))


def tree_sum(terms):
    while len(terms) > 1:
        terms = [terms[i] + terms[i + 1] for i in range(0, len(terms), 2)]
    return terms[0]


def stack_kernel(r_ref, src_ref, tab_ref, out_ref, wide, cross):
    wide[...] = src_ref[...].astype(F32)
    scale = 1.0 / math.sqrt(NB * 8)
    total = None
    for block in range(NB // LANES):
        half, inner = block // 5, block % 5
        columns = slice(LANES * inner, LANES * (inner + 1))
        real = [r_ref[32 * w : 32 * w + 32, LANES * block : LANES * (block + 1)] for w in range(8)]
        imag = [r_ref[32 * w : 32 * w + 32, NB + LANES * block : NB + LANES * (block + 1)] for w in range(8)]
        for source in range(8):
            member, e = source // 2, source % 2
            re_terms, im_terms = [], []
            for w in range(8):
                at_re = (member * 4 + half) * 16 + 2 * w + e
                at_im = (member * 4 + 2 + half) * 16 + 2 * w + e
                s_re = jnp.broadcast_to(wide[at_re : at_re + 1, columns], (32, LANES)).astype(BF16)
                s_im = jnp.broadcast_to(wide[at_im : at_im + 1, columns], (32, LANES)).astype(BF16)
                re_terms.append(real[w] * s_re + imag[w] * s_im)
                im_terms.append(imag[w] * s_re - real[w] * s_im)
            rows = slice(32 * source, 32 * source + 32)
            cross[rows, 2 * LANES * block : 2 * LANES * block + LANES] = tree_sum(re_terms)
            cross[rows, 2 * LANES * block + LANES : 2 * LANES * (block + 1)] = tree_sum(im_terms)
    out_ref[...] = jnp.dot(cross[...], tab_ref[...], preferred_element_type=F32) * scale


def stacked(receivers, sources):
    return pl.pallas_call(
        stack_kernel,
        out_shape=jax.ShapeDtypeStruct((256, LAGS), F32),
        scratch_shapes=[
            pltpu.VMEM((256, 640), F32),
            pltpu.VMEM((256, 2 * NB), BF16),
        ],
        compiler_params=pltpu.CompilerParams(vmem_limit_bytes=40 * 1024 * 1024),
        name="stack",
    )(receivers, sources, jnp.asarray(lag_table()))


def local(strain, gaps, source_block):
    block = source_block[0] % 32
    root_y, root_z = block // 8, block % 8
    whitened, scattered = spectra(strain.reshape(32, SAMPLES), gaps)
    receivers = lax.all_gather(whitened, ("x", "yl"), tiled=True)
    with jax.named_scope("scatter"):
        got = lax.all_to_all(scattered.reshape(16, 8, 640), ("z", "co"), 0, 0)
    mine = lax.dynamic_slice(got, (2 * root_z, 0, 0), (2, 8, 640)).reshape(8, 2, 640)
    with jax.named_scope("exchange"):
        sent = jnp.broadcast_to(mine[None], (4, 8, 2, 640)).reshape(32, 2, 640)
        got = lax.all_to_all(sent, ("yh", "x", "yl"), 0, 0)
    mine = lax.dynamic_slice(got, (8 * root_y, 0, 0), (8, 2, 640)).reshape(16, 640)
    with jax.named_scope("gather"):
        sent = jnp.broadcast_to(mine[None], (16, 16, 640))
        sources = lax.all_to_all(sent, ("z", "co"), 0, 0)
    return stacked(receivers, sources.reshape(256, 640)).reshape(8, 32, LAGS)


def solution(mesh):
    split = Mesh(mesh.devices.reshape(4, 8, 2, 4, 2), ("yh", "z", "co", "x", "yl"))
    chan, win = ("yh", "z", "co"), ("x", "yl")
    in_specs = (P(chan, win, None), P(chan, win), P())
    out_specs = P(win, chan, None)
    return jax.shard_map(local, mesh=split, in_specs=in_specs, out_specs=out_specs, check_vma=False)
```
